256 devices in a mesh: dp: 64 (over z, y, core), fsdp: 4 (over x).
Axes of the slice: x: 4, y: 4, z: 8, core: 2. Of those that a mesh axis runs over, the one named last changes fastest.
Arguments:
- projections: bfloat16 [512, 192, 4608], P(('dp', 'fsdp')), may hold values from -10 to 10
- residual_in: bfloat16 [512, 192, 1536], P(('dp', 'fsdp')), may hold values from -3 to 3
- velocity_target: bfloat16 [512, 128, 64], P(('dp', 'fsdp')), may hold values from -6 to 6
- out_weight: bfloat16 [1536, 1536], P(None, 'fsdp'), may hold values from -0.15625 to 0.15625
- final_weight: bfloat16 [1536, 64], replicated, may hold values from -0.15625 to 0.15625
- modulation: bfloat16 [32, 4608], replicated, may hold values from -3 to 3
- bucket_sizes: int32 [512], replicated, may hold values from 32 to 128, as said below
- liked: int32 [512], replicated, may hold values 0 or 1
- timesteps: int32 [512], replicated, may hold values from 0 to 31
- reference_error: float32 [512], replicated, may hold values from 0.7 to 5.7
- move_list: int32 [4, 32, 2], P('fsdp'), may hold values from 0 to 63, as said below
Outputs:
- out_weight_grad: float32 [1536, 1536], P('dp', 'fsdp')
- projection_grad: bfloat16 [768, 192, 4608], P(('dp', 'fsdp'))
- slot_loss: float32 [768], P(('dp', 'fsdp'))
The draws below stay inside these ranges and needn't reach their ends.
Inputs may be any that keep to these rules, and one draw needn't show every extreme that they name: `bucket_sizes`: a multiple of a quarter of 128. `move_list`: in each fsdp column every dp index stands in exactly one pair, as source or as destination; a pair's source has summed bucket sizes no smaller than its destination's.
All inputs are finite; a program needn't handle non-finite values.
Results may differ from the reference program's by a relative error of at most 0.012.
Values may be sent and summed in bfloat16 or wider, within the bound.
A program may use at most 128 MiB of HBM per device.

```python
import math
import jax
import jax.numpy as jnp
from jax import lax

D = 1536
HEADS = 12
HD = 128
PATCH = 64
TXT = 64
LMAX = 128
TBINS = 32
IMG_DEV = 2
SEQ = 192
SLOTS = 512
POST = 768
MOVES = 32
N_DP = 64
N_FSDP = 4
DEVICES = 256


def bucket_lengths(key):
    bucket_steps = jax.random.randint(key, (SLOTS,), 1, 5)
    bucket_steps = bucket_steps.at[0].set(4)
    return (bucket_steps * (LMAX // 4)).astype(jnp.int32)


def draw_bucket_sizes(key, part):
    lengths = bucket_lengths(key)
    return lengths


def draw_move_list(key, part):
    lengths = bucket_lengths(key)
    key = jax.random.fold_in(key, 7)
    device_loads = jnp.sum(lengths.reshape(N_DP, N_FSDP, IMG_DEV), axis=-1)
    tie_break = jax.random.permutation(key, N_DP).astype(jnp.int32)
    load_score = device_loads * N_DP + tie_break[:, None]
    ordering = jnp.argsort(-load_score, axis=0).astype(jnp.int32)
    sources = ordering[:MOVES]
    destinations = ordering[N_DP - MOVES:][::-1]
    return jnp.stack([sources.T, destinations.T], axis=-1).astype(jnp.int32)


def draw_projections(key, part):
    key = jax.random.fold_in(key, 11)
    full_shape = (SLOTS, TXT + LMAX, 3, HEADS, HD)
    base_values = jnp.clip(jax.random.normal(key, full_shape, jnp.float32), -4.0, 4.0)
    return base_values.reshape(SLOTS, TXT + LMAX, 3 * HEADS * HD).astype(jnp.bfloat16)


def draw_reference_error(key, part):
    key = jax.random.fold_in(key, 23)
    position = jnp.arange(SLOTS, dtype=jnp.float32) / (SLOTS - 1)
    spread = jax.random.uniform(key, (SLOTS,), jnp.float32, 0.9, 1.1)
    return (1.2 + 1.6 * position) * spread


def plant(array, rng, least, high):
    spot = [jax.random.randint(jax.random.fold_in(rng, axis), (), 0, length) for axis, length in enumerate(array.shape)]
    widest = array.shape.index(max(array.shape))
    neighbour = spot[:widest] + [(spot[widest] + 1) % array.shape[widest]] + spot[widest + 1:]
    return array.at[tuple(spot)].set(least).at[tuple(neighbour)].set(high)


def level_of(rng, dims, cuts, low, top_value):
    def one(dim, blocks):
        steps = jax.random.uniform(jax.random.fold_in(jax.random.fold_in(rng, 6), dim), (blocks,), jnp.float32, low / len(cuts), top_value / len(cuts))
        return jnp.repeat(jnp.exp(steps), dims[dim] // blocks).reshape((-1,) + (1,) * (len(dims) - dim - 1))

    level = one(*cuts[0])
    for cut in cuts[1:]:
        level = level * one(*cut)
    return level


def gaussian(own_key, shape, scale, most, shards=(), held_as=jnp.bfloat16):
    level = level_of(own_key, shape, shards, -0.22, 0.18) if shards else 1.0
    drawn = jax.random.normal(own_key, shape, jnp.float32) * scale * level
    return jnp.minimum(jnp.maximum(drawn, -most), most).astype(held_as)


def setup_inputs(seed: int = 0) -> dict:
    streams_of = jax.random.split(jax.random.key(seed), 12)
    projections = draw_projections(jax.random.fold_in(streams_of[11], 71), 0)
    residual_in = gaussian(streams_of[1], (SLOTS, SEQ, D), 0.5, 3.0, ((0, 256),))
    velocity_target = gaussian(streams_of[2], (SLOTS, LMAX, PATCH), 1.0, 6.0, ((0, 256),))
    out_weight = gaussian(streams_of[3], (HEADS * HD, D), (HEADS * HD) ** -0.5, 0.15625, ((1, 4),))
    final_weight = gaussian(streams_of[4], (D, PATCH), D ** -0.5, 0.15625)
    modulation = gaussian(streams_of[5], (TBINS, 3 * D), 0.5, 3.0)
    bucket_sizes = draw_bucket_sizes(jax.random.fold_in(streams_of[11], 71), 0)
    liked = plant((jax.random.randint(streams_of[7], (SLOTS,), 0, 2) < 1).astype(jnp.int32), jax.random.fold_in(streams_of[7], 1), 0, 1)
    timesteps = plant(jax.random.randint(streams_of[8], (SLOTS,), 0, TBINS), jax.random.fold_in(streams_of[8], 1), 0, TBINS - 1).astype(jnp.int32)
    reference_error = draw_reference_error(jax.random.fold_in(streams_of[11], 71), 0)
    move_list = draw_move_list(jax.random.fold_in(streams_of[11], 71), 0)
    return dict(projections=projections, residual_in=residual_in, velocity_target=velocity_target, out_weight=out_weight, final_weight=final_weight, modulation=modulation, bucket_sizes=bucket_sizes, liked=liked, timesteps=timesteps, reference_error=reference_error, move_list=move_list)


reward_scale = 2.0
loss_scale = 4096.0
norm_epsilon = 1e-06

def rounded(values_in):
    return lax.optimization_barrier(values_in.astype(jnp.bfloat16)).astype(jnp.float32)

def forward_image(projection, residual, target, image_size, stepped, modulation, out_weight, final_weight):
    split_heads = projection.astype(jnp.float32).reshape(TXT + LMAX, 3, HEADS, HD)
    queries = split_heads[TXT:, 0]
    key_rows = split_heads[:, 1]
    values = split_heads[:, 2]
    score_root = math.sqrt(HD)
    scores = jnp.einsum('qhd,khd->hqk', queries, key_rows) / score_root
    live_keys = jnp.arange(TXT + LMAX) < TXT + image_size
    scores = jnp.where(live_keys[None, None, :], scores, -1e+30)
    highest = lax.optimization_barrier(jnp.max(scores, axis=-1, keepdims=True))
    raised = jnp.exp(scores - highest)
    attention = raised / lax.optimization_barrier(jnp.sum(raised, axis=-1, keepdims=True))
    attention_low = rounded(attention)
    mixed_heads = jnp.einsum('hqk,khd->qhd', attention_low, values)
    mixed_heads = mixed_heads.reshape(LMAX, HEADS * HD).astype(jnp.bfloat16)
    branch = jnp.dot(mixed_heads, out_weight, preferred_element_type=jnp.float32)
    chosen = modulation[stepped].astype(jnp.float32)
    gate_values = chosen[:D]
    shift_values = chosen[D:2 * D]
    scale_values = chosen[2 * D:]
    residual_rows = residual[TXT:].astype(jnp.float32) + gate_values * branch
    centered = residual_rows - lax.optimization_barrier(jnp.mean(residual_rows, axis=-1, keepdims=True))
    inverse = lax.rsqrt(lax.optimization_barrier(jnp.mean(centered * centered, axis=-1, keepdims=True)) + norm_epsilon)
    unit_rows = centered * inverse
    normed = (unit_rows * (1.0 + scale_values) + shift_values).astype(jnp.bfloat16)
    predicted = jnp.dot(normed, final_weight, preferred_element_type=jnp.float32)
    valid_rows = (jnp.arange(LMAX) < image_size)[:, None]
    differ = jnp.where(valid_rows, predicted - target.astype(jnp.float32), 0.0)
    divisor = PATCH * image_size
    image_error = jnp.sum(differ * differ) / divisor
    return (queries, key_rows, values, attention, attention_low, mixed_heads, gate_values, scale_values, inverse, unit_rows, differ, divisor, image_error)

def backward_image(saved, slope, out_weight, final_weight):
    queries, key_rows, values, attention, attention_low, mixed_heads, gate_values, scale_values, inverse, unit_rows, differ, divisor, image_error = saved
    factor = slope * 2.0 / divisor
    d_predicted = (factor * differ).astype(jnp.bfloat16)
    d_normed = jnp.dot(d_predicted, final_weight.T, preferred_element_type=jnp.float32)
    scaled = d_normed * (1.0 + scale_values)
    d_residual = inverse * (scaled - lax.optimization_barrier(jnp.mean(scaled, axis=-1, keepdims=True)) - unit_rows * lax.optimization_barrier(jnp.mean(scaled * unit_rows, axis=-1, keepdims=True)))
    d_branch = (gate_values * d_residual).astype(jnp.bfloat16)
    weight_term = jnp.dot(mixed_heads.T, d_branch, preferred_element_type=jnp.float32)
    d_mixed = jnp.dot(d_branch, out_weight.T, preferred_element_type=jnp.float32)
    d_heads = rounded(d_mixed).reshape(LMAX, HEADS, HD)
    d_attention = jnp.einsum('qhd,khd->hqk', d_heads, values)
    row_totals = lax.optimization_barrier(jnp.sum(attention * d_attention, axis=-1, keepdims=True))
    d_scores = rounded(attention * (d_attention - row_totals) / math.sqrt(HD))
    d_queries = jnp.einsum('hqk,khd->qhd', d_scores, key_rows)
    d_keys = jnp.einsum('hqk,qhd->khd', d_scores, queries)
    d_values = jnp.einsum('hqk,qhd->khd', attention_low, d_heads)
    d_queries = jnp.concatenate([jnp.zeros((TXT, HEADS, HD), jnp.float32), d_queries], axis=0)
    image_grad = jnp.stack([d_queries, d_keys, d_values], axis=1).reshape(TXT + LMAX, 3 * HEADS * HD).astype(jnp.bfloat16)
    return (image_grad, weight_term)

def reference(projections, residual_in, velocity_target, out_weight, final_weight, modulation, bucket_sizes, liked, timesteps, reference_error, move_list):

    def forward_error(sample):
        projection, residual, target, image_size, stepped = sample
        return forward_image(projection, residual, target, image_size, stepped, modulation, out_weight, final_weight)[-1]
    errors = lax.map(forward_error, (projections, residual_in, velocity_target, bucket_sizes, timesteps))
    rewards = reward_scale * (reference_error - errors)
    anchor = jnp.sum(rewards) / SLOTS
    sign_values = (2 * liked - 1).astype(jnp.float32)
    sigmoid_values = jax.nn.sigmoid(sign_values * (rewards - anchor))
    losses = 1.0 - sigmoid_values
    slopes = loss_scale * reward_scale * sign_values * sigmoid_values * (1.0 - sigmoid_values)

    def backward_step(running, sample):
        projection, residual, target, image_size, stepped, slope = sample
        saved = forward_image(projection, residual, target, image_size, stepped, modulation, out_weight, final_weight)
        image_grad, weight_term = backward_image(saved, slope, out_weight, final_weight)
        return (running + weight_term, image_grad)
    initial = jnp.zeros((HEADS * HD, D), jnp.float32)
    weight_grad, image_grads = lax.scan(backward_step, initial, (projections, residual_in, velocity_target, bucket_sizes, timesteps, slopes))
    per_slot = IMG_DEV + 1
    grouped = bucket_sizes.reshape(DEVICES, IMG_DEV)
    ranking = grouped * IMG_DEV + (IMG_DEV - 1 - jnp.arange(IMG_DEV, dtype=jnp.int32))[None, :]
    longest = jnp.argmax(ranking, axis=1).astype(jnp.int32)
    shard_ids = jnp.arange(N_FSDP, dtype=jnp.int32)[:, None]
    source_dev = (move_list[:, :, 0] * N_FSDP + shard_ids).reshape(-1).astype(jnp.int32)
    target_dev = (move_list[:, :, 1] * N_FSDP + shard_ids).reshape(-1).astype(jnp.int32)
    heading = jnp.full((DEVICES,), -1, jnp.int32).at[source_dev].set(target_dev)
    image_ids = jnp.arange(SLOTS, dtype=jnp.int32)
    owner_dev = image_ids // IMG_DEV
    within = image_ids % IMG_DEV
    moving = (heading[owner_dev] >= 0) & (within == longest[owner_dev])
    placed = jnp.where(moving, heading[owner_dev] * per_slot + IMG_DEV, owner_dev * per_slot + within).astype(jnp.int32)
    projection_grad = jnp.zeros((POST, TXT + LMAX, 3 * HEADS * HD), jnp.bfloat16).at[placed].set(image_grads)
    slot_loss = jnp.zeros((POST,), jnp.float32).at[placed].set(losses)
    return (weight_grad, projection_grad, slot_loss)
```

```python
import functools
import math

import jax
import jax.numpy as jnp
from jax import lax
from jax.experimental import pallas as pl
from jax.experimental.pallas import tpu as pltpu
from jax.sharding import PartitionSpec as P

HEADS = 12
HD = 128
D = 1536
PATCH = 64
TXT = 64
LMAX = 128
SEQ = 192
IMAGES = 512
NZ, NY, NC, NX = 8, 4, 2, 4
COLS = D // NX
HALF = D // NC
PART = 24
GROUP = 4

REWARD_SCALE = 2.0
LOSS_SCALE = 4096.0
EPSILON = 1e-06
MESH = pl.DeviceIdType.MESH
F32 = jnp.float32
BF16 = jnp.bfloat16
VMEM_LIMIT = 56 * 1024 * 1024

ANY = pl.BlockSpec(memory_space=pl.ANY)
VMEM = pl.BlockSpec(memory_space=pltpu.VMEM)
SMEM = pl.BlockSpec(memory_space=pltpu.SMEM)


def place():
    rank = lax.axis_index("dp")
    return rank // (NY * NC), (rank // NC) % NY, rank % NC, lax.axis_index("fsdp")


def device(z, y, c, x):
    return ((z * NY + y) * NC + c, x)


def greet(partners):
    barrier = pltpu.get_barrier_semaphore()
    for partner in partners:
        pl.semaphore_signal(barrier, inc=1, device_id=partner, device_id_type=MESH)
    pl.semaphore_wait(barrier, len(partners))


def remote(src, dst, send, recv, target):
    return pltpu.make_async_remote_copy(
        src_ref=src, dst_ref=dst, send_sem=send, recv_sem=recv, device_id=target, device_id_type=MESH
    )


def dot(a, b, left, right):
    return lax.dot_general(a, b, (((left,), (right,)), ((), ())), preferred_element_type=F32)


def rows_of(start, size, step):
    return pl.ds(pl.multiple_of(start, step), size)


def longest(sizes, dev):
    return jnp.where(sizes[2 * dev] >= sizes[2 * dev + 1], 0, 1)


def image_kernel(
    proj_hbm, resid_hbm, weight_hbm, target, final, modulation, sizes, steps,
    grad_a, grad_b, mixed, d_branch, errors,
    proj, resid, weight, attention, branch, d_mixed,
    load_sem, w_send, w_recv, e_send, e_recv,
):
    z, y, c, x = place()
    dev = lax.axis_index("dp") * NX + x
    sibling = device(z, y, 1 - c, x)
    right, left = (x + 1) % NX, (x + NX - 1) % NX
    opposite = (x + 2) % NX
    others_x = [device(z, y, c, (x + k) % NX) for k in range(1, NX)]
    others_y = [device(z, (y + k) % NY, c, x) for k in range(1, NY)]
    others_z = [device((z + k) % NZ, y, c, x) for k in range(1, NZ)]

    load_proj = pltpu.make_async_copy(proj_hbm, proj, load_sem.at[0])
    load_proj.start()
    load_resid = pltpu.make_async_copy(resid_hbm.at[:, pl.ds(TXT, LMAX)], resid, load_sem.at[1])
    load_resid.start()
    load_weight = pltpu.make_async_copy(weight_hbm, weight.at[x], load_sem.at[2])
    load_weight.start()

    greet([sibling] + others_x + others_y + others_z)

    half = rows_of(c * HALF, HALF, 16)
    upper = rows_of(c * HALF, HALF // 2, 16)
    lower = rows_of(c * HALF + HALF // 2, HALF // 2, 16)
    mine = weight_hbm.at[half]
    to_right = remote(mine, weight.at[x, half], w_send.at[0], w_recv.at[0], device(z, y, c, right))
    to_left = remote(mine, weight.at[x, half], w_send.at[1], w_recv.at[1], device(z, y, c, left))
    to_right.start()
    to_left.start()
    load_proj.wait()

    first = longest(sizes, dev)
    root = 1.0 / math.sqrt(HD)
    key_index = lax.broadcasted_iota(jnp.int32, (LMAX, SEQ), 1)

    def head_forward(i, slot, size, h):
        cols = pl.multiple_of(h * HD, HD)
        q = proj[slot, pl.ds(TXT, LMAX), pl.ds(cols, HD)]
        k = proj[slot, :, pl.ds(D + cols, HD)]
        v = proj[slot, :, pl.ds(2 * D + cols, HD)]
        scores = dot(q, k, 1, 1) * root
        scores = jnp.where(key_index < TXT + size, scores, -1e30)
        raised = jnp.exp(scores - jnp.max(scores, axis=-1, keepdims=True))
        probs = raised * (1.0 / jnp.sum(raised, axis=-1, keepdims=True))
        attention[i, h] = probs
        mixed[rows_of(i * LMAX, LMAX, 16), pl.ds(cols, HD)] = dot(probs.astype(BF16), v, 1, 0).astype(BF16)

    def forward_group(n, carry):
        i = n // (HEADS // GROUP)
        slot = jnp.where(i == 0, first, 1 - first)
        size = sizes[2 * dev + slot]
        for j in range(GROUP):
            head_forward(i, slot, size, (n % (HEADS // GROUP)) * GROUP + j)
        return carry

    lax.fori_loop(0, 2 * HEADS // GROUP, forward_group, 0)

    to_right.wait_recv()
    on_right = remote(weight.at[left, upper], weight.at[left, upper], w_send.at[2], w_recv.at[2], device(z, y, c, right))
    on_right.start()
    to_left.wait_recv()
    on_left = remote(weight.at[right, lower], weight.at[right, lower], w_send.at[3], w_recv.at[3], device(z, y, c, left))
    on_left.start()
    across = []
    for n, owner in enumerate((left, right)):
        copy = remote(weight.at[owner, half], weight.at[owner, half], w_send.at[4 + n], w_recv.at[4 + n], sibling)
        copy.start()
        across.append(copy)
    load_weight.wait()
    load_resid.wait()

    def branch_part(owner):
        cols = rows_of(owner * COLS, COLS, 128)
        branch[:, cols] = dot(mixed[...], weight[owner], 1, 0)

    branch_part(x)
    across[0].wait_recv()
    branch_part(left)
    across[1].wait_recv()
    branch_part(right)
    on_right.wait_recv()
    on_left.wait_recv()
    last = remote(weight.at[opposite, half], weight.at[opposite, half], w_send.at[6], w_recv.at[6], sibling)
    last.start()
    last.wait_recv()
    branch_part(opposite)

    lane = lax.broadcasted_iota(jnp.int32, (1, 128), 1)
    row_index = lax.broadcasted_iota(jnp.int32, (PATCH, LMAX), 1)
    level = lax.broadcasted_iota(jnp.int32, (16, 32), 1)

    def image_middle(i, found):
        slot = jnp.where(i == 0, first, 1 - first)
        size = sizes[2 * dev + slot]
        chosen = dot((level == steps[2 * dev + slot]).astype(F32).astype(BF16), modulation[...], 1, 0)[0:1]
        gate = chosen[:, :D]
        shift = chosen[:, D : 2 * D]
        scale = 1.0 + chosen[:, 2 * D :]
        rows = rows_of(i * LMAX, LMAX, 16)
        residual = resid[slot].astype(F32) + gate * branch[rows]
        centered = residual - jnp.mean(residual, axis=-1, keepdims=True)
        inverse = lax.rsqrt(jnp.mean(centered * centered, axis=-1, keepdims=True) + EPSILON)
        unit = centered * inverse
        normed = (unit * scale + shift).astype(BF16)
        predicted = dot(final[...], normed, 1, 1)
        differ = jnp.where(row_index < size, predicted - target[slot].astype(F32), 0.0)
        divisor = jnp.full((1, 1), PATCH * size, jnp.int32).astype(F32)
        squares = jnp.sum(jnp.sum(differ * differ, axis=1, keepdims=True), axis=0, keepdims=True)
        d_predicted = (differ * (2.0 / divisor)).astype(BF16)
        scaled = dot(d_predicted, final[...], 0, 0) * scale
        d_residual = inverse * (
            scaled
            - jnp.mean(scaled, axis=-1, keepdims=True)
            - unit * jnp.mean(scaled * unit, axis=-1, keepdims=True)
        )
        d_branch[rows, :] = (gate * d_residual).astype(BF16)
        return found + jnp.where(lane == slot, squares / divisor, 0.0)

    errors[z, y, x, c] = lax.fori_loop(0, 2, image_middle, jnp.zeros((1, 128), F32))

    e_core = remote(errors.at[z, y, x, c], errors.at[z, y, x, c], e_send.at[0], e_recv.at[0], sibling)
    e_core.start()

    total = dot(d_branch[:, pl.ds(0, COLS)], weight[0], 1, 1)
    for owner in range(1, NX):
        total += dot(d_branch[:, pl.ds(owner * COLS, COLS)], weight[owner], 1, 1)
    d_mixed[...] = total.astype(BF16)

    e_core.wait_recv()
    e_x = [
        remote(errors.at[z, y, x], errors.at[z, y, x], e_send.at[k], e_recv.at[k], others_x[k - 1])
        for k in range(1, NX)
    ]
    for copy in e_x:
        copy.start()

    def head_backward(i, slot, h, grads):
        cols = pl.multiple_of(h * HD, HD)
        q = proj[slot, pl.ds(TXT, LMAX), pl.ds(cols, HD)]
        k = proj[slot, :, pl.ds(D + cols, HD)]
        v = proj[slot, :, pl.ds(2 * D + cols, HD)]
        d_head = d_mixed[rows_of(i * LMAX, LMAX, 16), pl.ds(cols, HD)]
        probs = attention[i, h]
        d_probs = dot(d_head, v, 1, 1)
        totals = jnp.sum(probs * d_probs, axis=-1, keepdims=True)
        d_scores = (probs * (d_probs - totals) * root).astype(BF16)
        side = h // (HEADS // 2)
        out_cols = rows_of((h % (HEADS // 2)) * HD, HD, 128)
        d_q = dot(d_scores, k, 1, 0).astype(BF16)
        d_k = dot(d_scores, q, 0, 0).astype(BF16)
        d_v = dot(probs.astype(BF16), d_head, 0, 0).astype(BF16)
        grads[side, 0:8, :, out_cols] = d_q.reshape(8, 16, HD)
        grads[side, 8:20, :, out_cols] = d_k.reshape(12, 16, HD)
        grads[side, 20:32, :, out_cols] = d_v.reshape(12, 16, HD)

    def backward(i, slot, grads):
        def group(n, carry):
            for j in range(GROUP):
                head_backward(i, slot, n * GROUP + j, grads)
            return carry

        lax.fori_loop(0, HEADS // GROUP, group, 0)

    backward(0, first, grad_a)

    for copy in e_x:
        copy.wait_recv()
    e_y = [
        remote(errors.at[z, y], errors.at[z, y], e_send.at[3 + k], e_recv.at[3 + k], others_y[k - 1])
        for k in range(1, NY)
    ]
    for copy in e_y:
        copy.start()

    backward(1, 1 - first, grad_b)

    for copy in e_y:
        copy.wait_recv()
    e_z = [
        remote(errors.at[z], errors.at[z], e_send.at[6 + k], e_recv.at[6 + k], others_z[k - 1])
        for k in range(1, NZ)
    ]
    for copy in e_z:
        copy.start()
    for copy in e_z:
        copy.wait_recv()
    for copy in [to_right, to_left, on_right, on_left, last, e_core] + across + e_x + e_y + e_z:
        copy.wait_send()


def image_pass(projections, residual_in, velocity_target, out_weight, final_weight, modulation, sizes, steps):
    grads = jax.ShapeDtypeStruct((2, 32, 16, HEADS // 2 * HD), BF16)
    return pl.pallas_call(
        image_kernel,
        name="images",
        out_shape=(
            grads,
            grads,
            jax.ShapeDtypeStruct((2 * LMAX, D), BF16),
            jax.ShapeDtypeStruct((2 * LMAX, D), BF16),
            jax.ShapeDtypeStruct((NZ, NY, NX, NC, 1, 128), F32),
        ),
        in_specs=[ANY, ANY, ANY, VMEM, VMEM, VMEM, SMEM, SMEM],
        out_specs=(VMEM,) * 5,
        scratch_shapes=[
            pltpu.VMEM((2, SEQ, 3 * D), BF16),
            pltpu.VMEM((2, LMAX, D), BF16),
            pltpu.VMEM((NX, D, COLS), BF16),
            pltpu.VMEM((2, HEADS, LMAX, SEQ), F32),
            pltpu.VMEM((2 * LMAX, D), F32),
            pltpu.VMEM((2 * LMAX, D), BF16),
            pltpu.SemaphoreType.DMA((3,)),
            pltpu.SemaphoreType.DMA((7,)),
            pltpu.SemaphoreType.DMA((7,)),
            pltpu.SemaphoreType.DMA((14,)),
            pltpu.SemaphoreType.DMA((14,)),
        ],
        compiler_params=pltpu.CompilerParams(
            collective_id=0, has_side_effects=True, vmem_limit_bytes=VMEM_LIMIT
        ),
        cost_estimate=pl.CostEstimate(flops=4_500_000_000, bytes_accessed=20_000_000, transcendentals=600_000),
    )(projections, residual_in, out_weight, velocity_target, final_weight, modulation, sizes, steps)


def anchor_of(errors, reference):
    flat = errors[...].reshape(NZ * NY * NX * NC, 128)
    total = jnp.sum(jnp.sum(flat, axis=0, keepdims=True), axis=1, keepdims=True)
    known = jnp.sum(jnp.sum(reference[...], axis=0, keepdims=True), axis=1, keepdims=True)
    return REWARD_SCALE * (known - total) / IMAGES


def loss_of(error_row, slot, known, liked, anchor):
    lane = lax.broadcasted_iota(jnp.int32, (1, 128), 1)
    error = jnp.sum(jnp.where(lane == slot, error_row, 0.0), axis=1, keepdims=True)
    sign = jnp.full((1, 1), 2 * liked - 1, jnp.int32).astype(F32)
    reward = REWARD_SCALE * (jnp.full((1, 1), known, F32) - error)
    sig = jax.nn.sigmoid(sign * (reward - anchor))
    return 1.0 - sig, LOSS_SCALE * REWARD_SCALE * sign * sig * (1.0 - sig)


def weight_kernel(
    mixed, d_branch, errors, reference, sizes, liked, known,
    out,
    scaled, term, core_send, core_recv, own, far_send, far_recv, near_send, near_recv, y_total,
    far_send_y, far_recv_y, near_send_y, near_recv_y, z_send, z_recv,
    c_sems, x_sems, y_sems, z_sems,
):
    z, y, c, x = place()
    dev = lax.axis_index("dp") * NX + x
    sibling = device(z, y, 1 - c, x)
    right_x, left_x = (x + 1) % NX, (x + NX - 1) % NX
    right_y, left_y = (y + 1) % NY, (y + NY - 1) % NY
    x_pair = (device(z, y, c, right_x), device(z, y, c, left_x))
    y_pair = (device(z, right_y, c, x), device(z, left_y, c, x))
    others_z = [device((z + k) % NZ, y, c, x) for k in range(1, NZ)]
    greet([sibling, *x_pair, *y_pair] + others_z)

    anchor = anchor_of(errors, reference)
    row = errors[z, y, x, c]
    first = longest(sizes, dev)
    for i in range(2):
        slot = first if i == 0 else 1 - first
        index = 2 * dev + slot
        _, slope = loss_of(row, slot, known[index], liked[index], anchor)
        rows = pl.ds(i * LMAX, LMAX)
        scaled[rows, :] = (d_branch[rows, :].astype(F32) * slope).astype(BF16)

    def make(owner):
        term[...] = dot(mixed[...], scaled[:, rows_of(owner * COLS, COLS, 128)], 0, 0)
        for yy in range(NY):
            for core, target in ((1 - c, core_send), (c, own)):
                parts = [
                    term[rows_of(((zz * NY + yy) * NC + core) * PART, PART, 8), :] for zz in range(NZ)
                ]
                block = jnp.concatenate(parts, axis=0)
                target[owner, pl.ds(yy * NZ * PART, NZ * PART), :] = block.astype(target.dtype)
        copy = remote(core_send.at[owner], core_recv.at[owner], c_sems.at[0, owner], c_sems.at[1, owner], sibling)
        copy.start()
        return copy

    opposite = (x + 2) % NX
    owners = (opposite, right_x, left_x, x)
    copies = [make(owner) for owner in owners]

    def chip_total(n):
        copies[n].wait_recv()
        own[owners[n]] = own[owners[n]] + core_recv[owners[n]].astype(F32)

    def ring(pair, sems, far, rights, lefts, far_out, far_in, near_out, near_in, size):
        middle = size // 2
        outer = []
        for n in range(2):
            far_out[n] = far(pl.ds(n * middle, middle)).astype(BF16)
            copy = remote(far_out.at[n], far_in.at[n], sems.at[0, n], sems.at[1, n], pair[n])
            copy.start()
            outer.append(copy)
        inner = []
        for n, near in ((0, rights), (1, lefts)):
            block = near()
            outer[n].wait_recv()
            for part in range(2):
                rows = pl.ds(part * middle, middle)
                piece = block(rows)
                if part == n:
                    piece = piece + far_in[n].astype(F32)
                near_out[n, rows, :] = piece.astype(BF16)
            copy = remote(near_out.at[n], near_in.at[n], sems.at[0, 2 + n], sems.at[1, 2 + n], pair[n])
            copy.start()
            inner.append(copy)
        return outer, inner

    chip_total(0)

    def near_x(n):
        def get():
            chip_total(n)
            return lambda rows: own[owners[n], rows, :]

        return get

    outer_x, inner_x = ring(
        x_pair, x_sems, lambda rows: own[opposite, rows, :], near_x(1), near_x(2),
        far_send, far_recv, near_send, near_recv, HALF,
    )
    chip_total(3)
    inner_x[0].wait_recv()
    inner_x[1].wait_recv()
    own[x] = own[x] + near_recv[0].astype(F32) + near_recv[1].astype(F32)

    strip = NZ * PART

    def y_rows(which, rows):
        return own[x, pl.ds(pl.multiple_of(which * strip, 16) + rows.start, rows.size), :]

    outer_y, inner_y = ring(
        y_pair, y_sems, lambda rows: y_rows((y + 2) % NY, rows),
        lambda: lambda rows: y_rows(right_y, rows), lambda: lambda rows: y_rows(left_y, rows),
        far_send_y, far_recv_y, near_send_y, near_recv_y, strip,
    )
    inner_y[0].wait_recv()
    inner_y[1].wait_recv()
    y_total[...] = (
        y_rows(y, pl.ds(0, strip)) + near_recv_y[0].astype(F32) + near_recv_y[1].astype(F32)
    )
    for zz in range(NZ):
        z_send[zz] = y_total[pl.ds(zz * PART, PART), :]
    z_copies = []
    for k in range(1, NZ):
        copy = remote(
            z_send.at[(z + k) % NZ], z_recv.at[k - 1], z_sems.at[0, k - 1], z_sems.at[1, k - 1], others_z[k - 1]
        )
        copy.start()
        z_copies.append(copy)
    total = z_send[z]
    for k, copy in enumerate(z_copies):
        copy.wait_recv()
        total = total + z_recv[k]
    out[...] = total
    for copy in copies + outer_x + inner_x + outer_y + inner_y + z_copies:
        copy.wait_send()


def weight_pass(mixed, d_branch, errors, reference, sizes, liked, known):
    strip = NZ * PART
    return pl.pallas_call(
        weight_kernel,
        name="weight",
        out_shape=jax.ShapeDtypeStruct((PART, COLS), F32),
        in_specs=[VMEM, VMEM, VMEM, VMEM, SMEM, SMEM, SMEM],
        out_specs=VMEM,
        scratch_shapes=[
            pltpu.VMEM((2 * LMAX, D), BF16),
            pltpu.VMEM((D, COLS), F32),
            pltpu.VMEM((NX, HALF, COLS), BF16),
            pltpu.VMEM((NX, HALF, COLS), BF16),
            pltpu.VMEM((NX, HALF, COLS), F32),
            pltpu.VMEM((2, HALF // 2, COLS), BF16),
            pltpu.VMEM((2, HALF // 2, COLS), BF16),
            pltpu.VMEM((2, HALF, COLS), BF16),
            pltpu.VMEM((2, HALF, COLS), BF16),
            pltpu.VMEM((strip, COLS), F32),
            pltpu.VMEM((2, strip // 2, COLS), BF16),
            pltpu.VMEM((2, strip // 2, COLS), BF16),
            pltpu.VMEM((2, strip, COLS), BF16),
            pltpu.VMEM((2, strip, COLS), BF16),
            pltpu.VMEM((NZ, PART, COLS), F32),
            pltpu.VMEM((NZ - 1, PART, COLS), F32),
            pltpu.SemaphoreType.DMA((2, NX)),
            pltpu.SemaphoreType.DMA((2, 4)),
            pltpu.SemaphoreType.DMA((2, 4)),
            pltpu.SemaphoreType.DMA((2, NZ - 1)),
        ],
        compiler_params=pltpu.CompilerParams(
            collective_id=1, has_side_effects=True, vmem_limit_bytes=VMEM_LIMIT
        ),
        cost_estimate=pl.CostEstimate(flops=1_200_000_000, bytes_accessed=60_000_000, transcendentals=10),
    )(mixed, d_branch, errors, reference, sizes, liked, known)


def place_kernel(rank_ref, moves, sizes, liked, known, grad_a, grad_b, arrived, errors, reference, out, losses):
    rank = rank_ref[0]
    x = rank_ref[1]
    dev = rank * NX + x
    slot = pl.program_id(0)

    def look(n, found):
        source, goal = moves[2 * n], moves[2 * n + 1]
        leaving, origin = found
        return jnp.where(source == rank, 1, leaving), jnp.where(goal == rank, source, origin)

    leaving, origin = lax.fori_loop(0, moves.shape[0] // 2, look, (jnp.int32(0), jnp.int32(-1)))
    anchor = anchor_of(errors, reference)
    first = longest(sizes, dev)
    is_new = slot == 2
    from_rank = jnp.where(is_new, jnp.maximum(origin, 0), rank)
    from_dev = from_rank * NX + x
    from_slot = jnp.where(is_new, longest(sizes, from_dev), slot)
    index = 2 * from_dev + from_slot
    row = errors[from_rank // (NY * NC), (from_rank // NC) % NY, x, from_rank % NC]
    loss, slope = loss_of(row, from_slot, known[index], liked[index], anchor)
    goes = jnp.logical_and(leaving == 1, slot == first)
    present = jnp.where(is_new, origin >= 0, jnp.logical_not(goes))
    losses[slot] = jnp.where(present, loss[0, 0], 0.0)

    wide = HEADS // 2 * HD

    def write(grads):
        for side in range(2):
            for base, low, count, rows in ((0, 0, 8, LMAX), (D, 8, 12, SEQ), (2 * D, 20, 12, SEQ)):
                block = grads[side, low : low + count].reshape(rows, wide).astype(F32) * slope
                out[0, SEQ - rows :, base + side * wide : base + (side + 1) * wide] = block.astype(BF16)
        out[0, :TXT, :D] = jnp.zeros((TXT, D), BF16)

    @pl.when(jnp.logical_not(present))
    def _():
        out[...] = jnp.zeros_like(out)

    @pl.when(jnp.logical_and(present, is_new))
    def _():
        write(arrived)

    @pl.when(jnp.logical_and(present, slot == first))
    def _():
        write(grad_a)

    @pl.when(jnp.logical_and(present, slot == 1 - first))
    def _():
        write(grad_b)


def place_pass(place_of, moves, sizes, liked, known, grad_a, grad_b, arrived, errors, reference):
    return pl.pallas_call(
        place_kernel,
        name="slots",
        grid=(3,),
        out_shape=(jax.ShapeDtypeStruct((3, SEQ, 3 * D), BF16), jax.ShapeDtypeStruct((3,), F32)),
        in_specs=[SMEM] * 5 + [VMEM] * 5,
        out_specs=(pl.BlockSpec((1, SEQ, 3 * D), lambda i: (i, 0, 0)), SMEM),
        compiler_params=pltpu.CompilerParams(vmem_limit_bytes=VMEM_LIMIT),
        cost_estimate=pl.CostEstimate(flops=3_000_000, bytes_accessed=10_000_000, transcendentals=10),
    )(place_of, moves, sizes, liked, known, grad_a, grad_b, arrived, errors, reference)


def local(
    projections, residual_in, velocity_target, out_weight, final_weight, modulation,
    bucket_sizes, liked, timesteps, reference_error, move_list,
):
    rank = lax.axis_index("dp")
    senders = lax.axis_size("dp")
    reference = reference_error.reshape(4, 128)
    moves = move_list.reshape(-1)
    place_of = jnp.stack([rank, lax.axis_index("fsdp")]).astype(jnp.int32)
    grad_a, grad_b, mixed, d_branch, errors = image_pass(
        projections, residual_in, jnp.swapaxes(velocity_target, 1, 2), out_weight, final_weight.T,
        modulation, bucket_sizes, timesteps,
    )
    spread = lax.all_to_all(
        grad_a.reshape(senders, 16, -1), "dp", split_axis=0, concat_axis=0, tiled=True
    )
    target_of = jnp.arange(senders, dtype=jnp.int32)[:, None] == move_list[0, :, 1][None, :]
    sender_rank = jnp.sum(jnp.where(target_of, move_list[0, :, 0][None, :], 0), axis=1)
    picked = jnp.take(spread, sender_rank, axis=0, mode="clip")
    arrived = lax.all_to_all(picked, "dp", split_axis=0, concat_axis=0, tiled=True)
    weight_grad = weight_pass(mixed, d_branch, errors, reference, bucket_sizes, liked, reference_error)
    projection_grad, slot_loss = place_pass(
        place_of, moves, bucket_sizes, liked, reference_error,
        grad_a, grad_b, arrived.reshape(grad_a.shape), errors, reference,
    )
    return (weight_grad, projection_grad, slot_loss)


def solution(mesh):
    in_specs = (
        P(("dp", "fsdp"), None, None),
        P(("dp", "fsdp"), None, None),
        P(("dp", "fsdp"), None, None),
        P(None, "fsdp"),
        P(),
        P(),
        P(),
        P(),
        P(),
        P(),
        P("fsdp", None, None),
    )
    out_specs = (P("dp", "fsdp"), P(("dp", "fsdp"), None, None), P(("dp", "fsdp")))
    return jax.shard_map(local, mesh=mesh, in_specs=in_specs, out_specs=out_specs, check_vma=False)
```

```python
import functools
import math

import jax
import jax.numpy as jnp
from jax import lax
from jax.experimental import pallas as pl
from jax.experimental.pallas import tpu as pltpu
from jax.sharding import PartitionSpec as P

HEADS = 12
HD = 128
D = 1536
PATCH = 64
TXT = 64
LMAX = 128
SEQ = 192
IMAGES = 512
NZ, NY, NC, NX = 8, 4, 2, 4
COLS = D // NX
HALF = D // NC
PART = 24
GROUP = 4
DP = NZ * NY * NC
EARLY = 8
LATE = HEADS - EARLY
TILE = 16
STRIDE = 27

REWARD_SCALE = 2.0
LOSS_SCALE = 4096.0
EPSILON = 1e-06
MESH = pl.DeviceIdType.MESH
F32 = jnp.float32
BF16 = jnp.bfloat16
VMEM_LIMIT = 56 * 1024 * 1024

PARTS = ((0, 0, 8, LMAX), (D, 8, 12, SEQ), (2 * D, 20, 12, SEQ))

ANY = pl.BlockSpec(memory_space=pl.ANY)
VMEM = pl.BlockSpec(memory_space=pltpu.VMEM)
SMEM = pl.BlockSpec(memory_space=pltpu.SMEM)


def place():
    rank = lax.axis_index("dp")
    return rank // (NY * NC), (rank // NC) % NY, rank % NC, lax.axis_index("fsdp")


def device(z, y, c, x):
    return ((z * NY + y) * NC + c, x)


def greet(partners):
    barrier = pltpu.get_barrier_semaphore()
    for partner in partners:
        pl.semaphore_signal(barrier, inc=1, device_id=partner, device_id_type=MESH)
    pl.semaphore_wait(barrier, len(partners))


def remote(src, dst, send, recv, target):
    return pltpu.make_async_remote_copy(
        src_ref=src, dst_ref=dst, send_sem=send, recv_sem=recv, device_id=target, device_id_type=MESH
    )


def dot(a, b, left, right):
    return lax.dot_general(a, b, (((left,), (right,)), ((), ())), preferred_element_type=F32)


def rows_of(start, size, step):
    return pl.ds(pl.multiple_of(start, step), size)


def longest(sizes, dev):
    return jnp.where(sizes[2 * dev] >= sizes[2 * dev + 1], 0, 1)


def anchor_of(errors, reference):
    flat = errors[...].reshape(NZ * NY * NX * NC, 128)
    total = jnp.sum(jnp.sum(flat, axis=0, keepdims=True), axis=1, keepdims=True)
    known = jnp.sum(jnp.sum(reference[...], axis=0, keepdims=True), axis=1, keepdims=True)
    return REWARD_SCALE * (known - total) / IMAGES


def loss_of(error_row, slot, known, liked, anchor):
    lane = lax.broadcasted_iota(jnp.int32, (1, 128), 1)
    error = jnp.sum(jnp.where(lane == slot, error_row, 0.0), axis=1, keepdims=True)
    sign = jnp.full((1, 1), 2 * liked - 1, jnp.int32).astype(F32)
    reward = REWARD_SCALE * (jnp.full((1, 1), known, F32) - error)
    sig = jax.nn.sigmoid(sign * (reward - anchor))
    return 1.0 - sig, LOSS_SCALE * REWARD_SCALE * sign * sig * (1.0 - sig)


def spread(stage, landed, sems, z, y, c, x):
    rank = (z * NY + y) * NC + c

    def step(n, carry):
        k = (n * STRIDE) % DP
        goal = (((z + k // (NY * NC)) % NZ) * NY + (y + (k // NC) % NY) % NY) * NC + (c + k % NC) % NC
        remote(stage.at[goal], landed.at[rank], sems.at[0], sems.at[1], (goal, x)).start()
        return carry

    lax.fori_loop(1, DP, step, 0)
    landed[rank] = stage[rank]
    most = pl.ds(0, DP - 1)
    return remote(stage.at[most], landed.at[most], sems.at[0], sems.at[1], ((rank + 1) % DP, x))


def pick(landed, stage, senders):
    def step(d, carry):
        stage[d] = landed[senders[d]]
        return carry

    lax.fori_loop(0, DP, step, 0)


def step_kernel(
    proj_hbm, resid_hbm, weight_hbm, target, final, modulation, reference, sizes, steps, liked, known, senders,
    grad_a, grad_b, grad_c, errors, out,
    proj, resid, weight, attention, branch, d_mixed, mixed, d_branch,
    stage_a, first_a, second_a, final_a, stage_b, first_b, second_b, final_b,
    scaled, term, core_send, core_recv, own, far_send, far_recv, near_send, near_recv, y_total,
    far_send_y, far_recv_y, near_send_y, near_recv_y, z_send, z_recv,
    load_sem, w_send, w_recv, e_send, e_recv, move_sems, c_sems, x_sems, y_sems, z_sems,
):
    z, y, c, x = place()
    rank = lax.axis_index("dp")
    dev = rank * NX + x
    sibling = device(z, y, 1 - c, x)
    right, left = (x + 1) % NX, (x + NX - 1) % NX
    opposite = (x + 2) % NX
    right_y, left_y = (y + 1) % NY, (y + NY - 1) % NY
    others_x = [device(z, y, c, (x + k) % NX) for k in range(1, NX)]
    others_y = [device(z, (y + k) % NY, c, x) for k in range(1, NY)]
    others_z = [device((z + k) % NZ, y, c, x) for k in range(1, NZ)]
    x_pair = (device(z, y, c, right), device(z, y, c, left))
    y_pair = (device(z, right_y, c, x), device(z, left_y, c, x))

    load_proj = pltpu.make_async_copy(proj_hbm, proj, load_sem.at[0])
    load_proj.start()
    load_resid = pltpu.make_async_copy(resid_hbm.at[:, pl.ds(TXT, LMAX)], resid, load_sem.at[1])
    load_resid.start()
    load_weight = pltpu.make_async_copy(weight_hbm, weight.at[x], load_sem.at[2])
    load_weight.start()

    barrier = pltpu.get_barrier_semaphore()
    for partner in others_x:
        pl.semaphore_signal(barrier, inc=1, device_id=partner, device_id_type=MESH)

    def hello(k, carry):
        pl.semaphore_signal(barrier, inc=1, device_id=((rank + k) % DP, x), device_id_type=MESH)
        return carry

    lax.fori_loop(1, DP, hello, 0)
    pl.semaphore_wait(barrier, DP - 1 + NX - 1)

    half = rows_of(c * HALF, HALF, 16)
    upper = rows_of(c * HALF, HALF // 2, 16)
    lower = rows_of(c * HALF + HALF // 2, HALF // 2, 16)
    mine = weight_hbm.at[half]
    to_right = remote(mine, weight.at[x, half], w_send.at[0], w_recv.at[0], x_pair[0])
    to_left = remote(mine, weight.at[x, half], w_send.at[1], w_recv.at[1], x_pair[1])
    to_right.start()
    to_left.start()
    load_proj.wait()

    first = longest(sizes, dev)
    narrow = EARLY // 2 * HD
    for side in range(2):
        for base, low, count, rows in PARTS:
            block = proj[first, SEQ - rows :, base + side * narrow : base + (side + 1) * narrow]
            stage_a[side * 32 + low : side * 32 + low + count] = block.reshape(count, TILE, narrow)
    move_1a = spread(stage_a, first_a, move_sems.at[0], z, y, c, x)

    root = 1.0 / math.sqrt(HD)
    key_index = lax.broadcasted_iota(jnp.int32, (LMAX, SEQ), 1)

    def softmax(q, k, size):
        scores = dot(q, k, 1, 1) * root
        scores = jnp.where(key_index < TXT + size, scores, -1e30)
        raised = jnp.exp(scores - jnp.max(scores, axis=-1, keepdims=True))
        return raised * (1.0 / jnp.sum(raised, axis=-1, keepdims=True))

    def gradients(q, k, v, probs, d_head):
        d_probs = dot(d_head, v, 1, 1)
        totals = jnp.sum(probs * d_probs, axis=-1, keepdims=True)
        d_scores = (probs * (d_probs - totals) * root).astype(BF16)
        return (
            dot(d_scores, k, 1, 0).astype(BF16),
            dot(d_scores, q, 0, 0).astype(BF16),
            dot(probs.astype(BF16), d_head, 0, 0).astype(BF16),
        )

    def head_forward(i, slot, size, h):
        cols = pl.multiple_of(h * HD, HD)
        q = proj[slot, pl.ds(TXT, LMAX), pl.ds(cols, HD)]
        k = proj[slot, :, pl.ds(D + cols, HD)]
        v = proj[slot, :, pl.ds(2 * D + cols, HD)]
        probs = softmax(q, k, size)
        attention[i, h] = probs
        mixed[rows_of(i * LMAX, LMAX, 16), pl.ds(cols, HD)] = dot(probs.astype(BF16), v, 1, 0).astype(BF16)

    def forward_group(n, carry):
        i = n // (HEADS // GROUP)
        slot = jnp.where(i == 0, first, 1 - first)
        size = sizes[2 * dev + slot]
        for j in range(GROUP):
            head_forward(i, slot, size, (n % (HEADS // GROUP)) * GROUP + j)
        return carry

    lax.fori_loop(0, 2 * HEADS // GROUP, forward_group, 0)

    to_right.wait_recv()
    on_right = remote(weight.at[left, upper], weight.at[left, upper], w_send.at[2], w_recv.at[2], x_pair[0])
    on_right.start()
    to_left.wait_recv()
    on_left = remote(weight.at[right, lower], weight.at[right, lower], w_send.at[3], w_recv.at[3], x_pair[1])
    on_left.start()
    across = []
    for n, owner in enumerate((left, right)):
        copy = remote(weight.at[owner, half], weight.at[owner, half], w_send.at[4 + n], w_recv.at[4 + n], sibling)
        copy.start()
        across.append(copy)
    load_weight.wait()
    load_resid.wait()

    def branch_part(owner):
        cols = rows_of(owner * COLS, COLS, 128)
        branch[:, cols] = dot(mixed[...], weight[owner], 1, 0)

    branch_part(x)
    across[0].wait_recv()
    branch_part(left)
    across[1].wait_recv()
    branch_part(right)
    on_right.wait_recv()
    on_left.wait_recv()
    last = remote(weight.at[opposite, half], weight.at[opposite, half], w_send.at[6], w_recv.at[6], sibling)
    last.start()
    last.wait_recv()
    branch_part(opposite)

    lane = lax.broadcasted_iota(jnp.int32, (1, 128), 1)
    row_index = lax.broadcasted_iota(jnp.int32, (PATCH, LMAX), 1)
    level = lax.broadcasted_iota(jnp.int32, (16, 32), 1)

    def image_middle(i, found):
        slot = jnp.where(i == 0, first, 1 - first)
        size = sizes[2 * dev + slot]
        chosen = dot((level == steps[2 * dev + slot]).astype(F32).astype(BF16), modulation[...], 1, 0)[0:1]
        gate = chosen[:, :D]
        shift = chosen[:, D : 2 * D]
        scale = 1.0 + chosen[:, 2 * D :]
        rows = rows_of(i * LMAX, LMAX, 16)
        residual = resid[slot].astype(F32) + gate * branch[rows]
        centered = residual - jnp.mean(residual, axis=-1, keepdims=True)
        inverse = lax.rsqrt(jnp.mean(centered * centered, axis=-1, keepdims=True) + EPSILON)
        unit = centered * inverse
        normed = (unit * scale + shift).astype(BF16)
        predicted = dot(final[...], normed, 1, 1)
        differ = jnp.where(row_index < size, predicted - target[slot].astype(F32), 0.0)
        divisor = jnp.full((1, 1), PATCH * size, jnp.int32).astype(F32)
        squares = jnp.sum(jnp.sum(differ * differ, axis=1, keepdims=True), axis=0, keepdims=True)
        d_predicted = (differ * (2.0 / divisor)).astype(BF16)
        scaled = dot(d_predicted, final[...], 0, 0) * scale
        d_residual = inverse * (
            scaled
            - jnp.mean(scaled, axis=-1, keepdims=True)
            - unit * jnp.mean(scaled * unit, axis=-1, keepdims=True)
        )
        d_branch[rows, :] = (gate * d_residual).astype(BF16)
        return found + jnp.where(lane == slot, squares / divisor, 0.0)

    errors[z, y, x, c] = lax.fori_loop(0, 2, image_middle, jnp.zeros((1, 128), F32))

    e_core = remote(errors.at[z, y, x, c], errors.at[z, y, x, c], e_send.at[0], e_recv.at[0], sibling)
    e_core.start()

    total = dot(d_branch[:, pl.ds(0, COLS)], weight[0], 1, 1)
    for owner in range(1, NX):
        total += dot(d_branch[:, pl.ds(owner * COLS, COLS)], weight[owner], 1, 1)
    d_mixed[...] = total.astype(BF16)

    e_core.wait_recv()
    e_x = [
        remote(errors.at[z, y, x], errors.at[z, y, x], e_send.at[k], e_recv.at[k], others_x[k - 1])
        for k in range(1, NX)
    ]
    for copy in e_x:
        copy.start()

    def head_backward(i, slot, h, grads, moved=False):
        cols = h * HD if moved else pl.multiple_of(h * HD, HD)
        q = proj[slot, pl.ds(TXT, LMAX), pl.ds(cols, HD)]
        k = proj[slot, :, pl.ds(D + cols, HD)]
        v = proj[slot, :, pl.ds(2 * D + cols, HD)]
        d_head = d_mixed[rows_of(i * LMAX, LMAX, 16), pl.ds(cols, HD)]
        side = h // (HEADS // 2)
        out_cols = pl.ds((h % (HEADS // 2)) * HD, HD) if moved else rows_of((h % (HEADS // 2)) * HD, HD, 128)
        d_q, d_k, d_v = gradients(q, k, v, attention[i, h], d_head)
        if moved:
            pair, place_in = (h - EARLY) // 2, pl.ds((h - EARLY) % 2 * HD, HD)
            for low, count, block in ((0, 8, d_q), (8, 12, d_k), (20, 12, d_v)):
                for n in range(count):
                    stage_b[2 * (low + n) + pair, :, place_in] = block[n * TILE : (n + 1) * TILE]
        grads[side, 0:8, :, out_cols] = d_q.reshape(8, 16, HD)
        grads[side, 8:20, :, out_cols] = d_k.reshape(12, 16, HD)
        grads[side, 20:32, :, out_cols] = d_v.reshape(12, 16, HD)

    for h in range(EARLY, HEADS):
        head_backward(0, first, h, grad_a, moved=True)
    for h in range(EARLY):
        for n in range(LMAX // TILE):
            stage_b[n * EARLY + h, :, pl.ds(2 * HD, HD)] = d_mixed[pl.ds(n * TILE, TILE), pl.ds(h * HD, HD)]

    for copy in e_x:
        copy.wait_recv()
    e_y = [
        remote(errors.at[z, y], errors.at[z, y], e_send.at[3 + k], e_recv.at[3 + k], others_y[k - 1])
        for k in range(1, NY)
    ]
    for copy in e_y:
        copy.start()

    move_1a.wait_recv()
    pick(first_a, second_a, senders)

    for copy in e_y:
        copy.wait_recv()
    e_z = [
        remote(errors.at[z], errors.at[z], e_send.at[6 + k], e_recv.at[6 + k], others_z[k - 1])
        for k in range(1, NZ)
    ]
    for copy in e_z:
        copy.start()
    move_2a = spread(second_a, final_a, move_sems.at[1], z, y, c, x)
    move_1b = spread(stage_b, first_b, move_sems.at[2], z, y, c, x)

    def backward(i, slot, grads, groups):
        def group(n, carry):
            for j in range(GROUP):
                head_backward(i, slot, n * GROUP + j, grads)
            return carry

        lax.fori_loop(0, groups, group, 0)

    backward(0, first, grad_a, EARLY // GROUP)
    backward(1, 1 - first, grad_b, HEADS // GROUP)

    for copy in e_z:
        copy.wait_recv()

    anchor = anchor_of(errors, reference)
    row = errors[z, y, x, c]
    for i in range(2):
        slot = first if i == 0 else 1 - first
        index = 2 * dev + slot
        _, slope = loss_of(row, slot, known[index], liked[index], anchor)
        rows = pl.ds(i * LMAX, LMAX)
        scaled[rows, :] = (d_branch[rows, :].astype(F32) * slope).astype(BF16)

    from_dev = senders[rank] * NX + x
    third_size = sizes[2 * from_dev + longest(sizes, from_dev)]

    def third_rows(h, part):
        _, low, count, rows = PARTS[part]
        base = h // (EARLY // 2) * 32 + low
        return final_a[base : base + count, :, pl.ds(h % (EARLY // 2) * HD, HD)].reshape(rows, HD)

    def third_forward():
        move_2a.wait_recv()
        for h in range(EARLY):
            attention[0, h] = softmax(third_rows(h, 0), third_rows(h, 1), third_size)

    def third_backward(h):
        d_head = jnp.concatenate(
            [final_b[n * EARLY + h, :, pl.ds(2 * HD, HD)] for n in range(LMAX // TILE)], axis=0
        )
        side, out_cols = h // (HEADS // 2), pl.ds((h % (HEADS // 2)) * HD, HD)
        q, k, v = (third_rows(h, part) for part in range(3))
        for (_, low, count, _), block in zip(PARTS, gradients(q, k, v, attention[0, h], d_head)):
            grad_c[side, low : low + count, :, out_cols] = block.reshape(count, TILE, HD)

    def make(owner):
        term[...] = dot(mixed[...], scaled[:, rows_of(owner * COLS, COLS, 128)], 0, 0)
        for yy in range(NY):
            for core, target in ((1 - c, core_send), (c, own)):
                parts = [
                    term[rows_of(((zz * NY + yy) * NC + core) * PART, PART, 8), :] for zz in range(NZ)
                ]
                block = jnp.concatenate(parts, axis=0)
                target[owner, pl.ds(yy * NZ * PART, NZ * PART), :] = block.astype(target.dtype)
        copy = remote(core_send.at[owner], core_recv.at[owner], c_sems.at[0, owner], c_sems.at[1, owner], sibling)
        copy.start()
        return copy

    owners = (opposite, right, left, x)
    copies = [make(owner) for owner in owners]

    def chip_total(n):
        copies[n].wait_recv()
        own[owners[n]] = own[owners[n]] + core_recv[owners[n]].astype(F32)

    def ring(pair, sems, far, rights, lefts, far_out, far_in, near_out, near_in, size, between):
        middle = size // 2
        outer = []
        for n in range(2):
            far_out[n] = far(pl.ds(n * middle, middle)).astype(BF16)
            copy = remote(far_out.at[n], far_in.at[n], sems.at[0, n], sems.at[1, n], pair[n])
            copy.start()
            outer.append(copy)
        between()
        inner = []
        for n, near in ((0, rights), (1, lefts)):
            block = near()
            outer[n].wait_recv()
            for part in range(2):
                rows = pl.ds(part * middle, middle)
                piece = block(rows)
                if part == n:
                    piece = piece + far_in[n].astype(F32)
                near_out[n, rows, :] = piece.astype(BF16)
            copy = remote(near_out.at[n], near_in.at[n], sems.at[0, 2 + n], sems.at[1, 2 + n], pair[n])
            copy.start()
            inner.append(copy)
        return outer, inner

    chip_total(0)

    def near_x(n):
        def get():
            chip_total(n)
            return lambda rows: own[owners[n], rows, :]

        return get

    outer_x, inner_x = ring(
        x_pair, x_sems, lambda rows: own[opposite, rows, :], near_x(1), near_x(2),
        far_send, far_recv, near_send, near_recv, HALF, third_forward,
    )
    move_1b.wait_recv()
    pick(first_b, second_b, senders)
    move_2b = spread(second_b, final_b, move_sems.at[3], z, y, c, x)
    chip_total(3)
    inner_x[0].wait_recv()
    inner_x[1].wait_recv()
    own[x] = own[x] + near_recv[0].astype(F32) + near_recv[1].astype(F32)

    strip = NZ * PART

    def y_rows(which, rows):
        return own[x, pl.ds(pl.multiple_of(which * strip, 16) + rows.start, rows.size), :]

    outer_y, inner_y = ring(
        y_pair, y_sems, lambda rows: y_rows((y + 2) % NY, rows),
        lambda: lambda rows: y_rows(right_y, rows), lambda: lambda rows: y_rows(left_y, rows),
        far_send_y, far_recv_y, near_send_y, near_recv_y, strip, lambda: None,
    )
    inner_y[0].wait_recv()
    inner_y[1].wait_recv()
    y_total[...] = (
        y_rows(y, pl.ds(0, strip)) + near_recv_y[0].astype(F32) + near_recv_y[1].astype(F32)
    )
    for zz in range(NZ):
        z_send[zz] = y_total[pl.ds(zz * PART, PART), :]
    z_copies = []
    for k in range(1, NZ):
        copy = remote(
            z_send.at[(z + k) % NZ], z_recv.at[k - 1], z_sems.at[0, k - 1], z_sems.at[1, k - 1], others_z[k - 1]
        )
        copy.start()
        z_copies.append(copy)
    total = z_send[z]
    for k, copy in enumerate(z_copies):
        copy.wait_recv()
        total = total + z_recv[k]
    out[...] = total

    move_2b.wait_recv()
    for n in range(EARLY // GROUP):
        for j in range(GROUP):
            third_backward(n * GROUP + j)
    for h in range(EARLY, HEADS):
        pair, place_in = (h - EARLY) // 2, pl.ds((h - EARLY) % 2 * HD, HD)
        out_cols = pl.ds((h % (HEADS // 2)) * HD, HD)
        for n in range(32):
            grad_c[h // (HEADS // 2), n, :, out_cols] = final_b[2 * n + pair, :, place_in]

    for copy in copies + outer_x + inner_x + outer_y + inner_y + z_copies:
        copy.wait_send()
    for copy in [to_right, to_left, on_right, on_left, last, e_core] + across + e_x + e_y + e_z:
        copy.wait_send()
    for copy in (move_1a, move_2a, move_1b, move_2b):
        copy.wait_send()


def step_pass(
    projections, residual_in, velocity_target, out_weight, final_weight, modulation,
    reference, sizes, steps, liked, known, senders,
):
    strip = NZ * PART
    grads = jax.ShapeDtypeStruct((2, 32, TILE, HEADS // 2 * HD), BF16)
    chunks_a = pltpu.VMEM((DP, TILE, EARLY // 2 * HD), BF16)
    chunks_b = pltpu.VMEM((DP, TILE, 3 * HD), BF16)
    return pl.pallas_call(
        step_kernel,
        name="step",
        out_shape=(
            grads,
            grads,
            grads,
            jax.ShapeDtypeStruct((NZ, NY, NX, NC, 1, 128), F32),
            jax.ShapeDtypeStruct((PART, COLS), F32),
        ),
        in_specs=[ANY, ANY, ANY, VMEM, VMEM, VMEM, VMEM] + [SMEM] * 5,
        out_specs=(VMEM,) * 5,
        scratch_shapes=[
            pltpu.VMEM((2, SEQ, 3 * D), BF16),
            pltpu.VMEM((2, LMAX, D), BF16),
            pltpu.VMEM((NX, D, COLS), BF16),
            pltpu.VMEM((2, HEADS, LMAX, SEQ), F32),
            pltpu.VMEM((2 * LMAX, D), F32),
            pltpu.VMEM((2 * LMAX, D), BF16),
            pltpu.VMEM((2 * LMAX, D), BF16),
            pltpu.VMEM((2 * LMAX, D), BF16),
            *[chunks_a] * 4,
            *[chunks_b] * 4,
            pltpu.VMEM((2 * LMAX, D), BF16),
            pltpu.VMEM((D, COLS), F32),
            pltpu.VMEM((NX, HALF, COLS), BF16),
            pltpu.VMEM((NX, HALF, COLS), BF16),
            pltpu.VMEM((NX, HALF, COLS), F32),
            pltpu.VMEM((2, HALF // 2, COLS), BF16),
            pltpu.VMEM((2, HALF // 2, COLS), BF16),
            pltpu.VMEM((2, HALF, COLS), BF16),
            pltpu.VMEM((2, HALF, COLS), BF16),
            pltpu.VMEM((strip, COLS), F32),
            pltpu.VMEM((2, strip // 2, COLS), BF16),
            pltpu.VMEM((2, strip // 2, COLS), BF16),
            pltpu.VMEM((2, strip, COLS), BF16),
            pltpu.VMEM((2, strip, COLS), BF16),
            pltpu.VMEM((NZ, PART, COLS), F32),
            pltpu.VMEM((NZ - 1, PART, COLS), F32),
            pltpu.SemaphoreType.DMA((3,)),
            pltpu.SemaphoreType.DMA((7,)),
            pltpu.SemaphoreType.DMA((7,)),
            pltpu.SemaphoreType.DMA((14,)),
            pltpu.SemaphoreType.DMA((14,)),
            pltpu.SemaphoreType.DMA((4, 2)),
            pltpu.SemaphoreType.DMA((2, NX)),
            pltpu.SemaphoreType.DMA((2, 4)),
            pltpu.SemaphoreType.DMA((2, 4)),
            pltpu.SemaphoreType.DMA((2, NZ - 1)),
        ],
        compiler_params=pltpu.CompilerParams(
            collective_id=0, has_side_effects=True, vmem_limit_bytes=VMEM_LIMIT
        ),
        cost_estimate=pl.CostEstimate(flops=5_700_000_000, bytes_accessed=20_000_000, transcendentals=800_000),
    )(
        projections, residual_in, out_weight, velocity_target, final_weight, modulation,
        reference, sizes, steps, liked, known, senders,
    )


def place_kernel(rank_ref, moves, sizes, liked, known, grad_a, grad_b, arrived, errors, reference, out, losses):
    rank = rank_ref[0]
    x = rank_ref[1]
    dev = rank * NX + x
    slot = pl.program_id(0)

    def look(n, found):
        source, goal = moves[2 * n], moves[2 * n + 1]
        leaving, origin = found
        return jnp.where(source == rank, 1, leaving), jnp.where(goal == rank, source, origin)

    leaving, origin = lax.fori_loop(0, moves.shape[0] // 2, look, (jnp.int32(0), jnp.int32(-1)))
    anchor = anchor_of(errors, reference)
    first = longest(sizes, dev)
    is_new = slot == 2
    from_rank = jnp.where(is_new, jnp.maximum(origin, 0), rank)
    from_dev = from_rank * NX + x
    from_slot = jnp.where(is_new, longest(sizes, from_dev), slot)
    index = 2 * from_dev + from_slot
    row = errors[from_rank // (NY * NC), (from_rank // NC) % NY, x, from_rank % NC]
    loss, slope = loss_of(row, from_slot, known[index], liked[index], anchor)
    goes = jnp.logical_and(leaving == 1, slot == first)
    present = jnp.where(is_new, origin >= 0, jnp.logical_not(goes))
    losses[slot] = jnp.where(present, loss[0, 0], 0.0)

    wide = HEADS // 2 * HD

    def write(grads):
        for side in range(2):
            for base, low, count, rows in PARTS:
                block = grads[side, low : low + count].reshape(rows, wide).astype(F32) * slope
                out[0, SEQ - rows :, base + side * wide : base + (side + 1) * wide] = block.astype(BF16)
        out[0, :TXT, :D] = jnp.zeros((TXT, D), BF16)

    @pl.when(jnp.logical_not(present))
    def _():
        out[...] = jnp.zeros_like(out)

    @pl.when(jnp.logical_and(present, is_new))
    def _():
        write(arrived)

    @pl.when(jnp.logical_and(present, slot == first))
    def _():
        write(grad_a)

    @pl.when(jnp.logical_and(present, slot == 1 - first))
    def _():
        write(grad_b)


def place_pass(place_of, moves, sizes, liked, known, grad_a, grad_b, arrived, errors, reference):
    return pl.pallas_call(
        place_kernel,
        name="slots",
        grid=(3,),
        out_shape=(jax.ShapeDtypeStruct((3, SEQ, 3 * D), BF16), jax.ShapeDtypeStruct((3,), F32)),
        in_specs=[SMEM] * 5 + [VMEM] * 5,
        out_specs=(pl.BlockSpec((1, SEQ, 3 * D), lambda i: (i, 0, 0)), SMEM),
        compiler_params=pltpu.CompilerParams(vmem_limit_bytes=VMEM_LIMIT),
        cost_estimate=pl.CostEstimate(flops=3_000_000, bytes_accessed=10_000_000, transcendentals=10),
    )(place_of, moves, sizes, liked, known, grad_a, grad_b, arrived, errors, reference)


def local(
    projections, residual_in, velocity_target, out_weight, final_weight, modulation,
    bucket_sizes, liked, timesteps, reference_error, move_list,
):
    rank = lax.axis_index("dp")
    senders = lax.axis_size("dp")
    reference = reference_error.reshape(4, 128)
    moves = move_list.reshape(-1)
    place_of = jnp.stack([rank, lax.axis_index("fsdp")]).astype(jnp.int32)
    target_of = jnp.arange(senders, dtype=jnp.int32)[:, None] == move_list[0, :, 1][None, :]
    sender_rank = jnp.sum(jnp.where(target_of, move_list[0, :, 0][None, :], 0), axis=1)
    grad_a, grad_b, grad_c, errors, weight_grad = step_pass(
        projections, residual_in, jnp.swapaxes(velocity_target, 1, 2), out_weight, final_weight.T,
        modulation, reference, bucket_sizes, timesteps, liked, reference_error, sender_rank,
    )
    projection_grad, slot_loss = place_pass(
        place_of, moves, bucket_sizes, liked, reference_error,
        grad_a, grad_b, grad_c, errors, reference,
    )
    return (weight_grad, projection_grad, slot_loss)


def solution(mesh):
    in_specs = (
        P(("dp", "fsdp"), None, None),
        P(("dp", "fsdp"), None, None),
        P(("dp", "fsdp"), None, None),
        P(None, "fsdp"),
        P(),
        P(),
        P(),
        P(),
        P(),
        P(),
        P("fsdp", None, None),
    )
    out_specs = (P("dp", "fsdp"), P(("dp", "fsdp"), None, None), P(("dp", "fsdp")))
    return jax.shard_map(local, mesh=mesh, in_specs=in_specs, out_specs=out_specs, check_vma=False)
```

```python
import functools
import math

import jax
import jax.numpy as jnp
from jax import lax
from jax.experimental import pallas as pl
from jax.experimental.pallas import tpu as pltpu
from jax.sharding import PartitionSpec as P

HEADS = 12
HD = 128
D = 1536
PATCH = 64
TXT = 64
LMAX = 128
SEQ = 192
IMAGES = 512
NZ, NY, NC, NX = 8, 4, 2, 4
COLS = D // NX
HALF = D // NC
PART = 24
STRIP = NZ // 2 * PART
BLOCK = NY * STRIP
GROUP = 4
DP = NZ * NY * NC
EARLY = 8
TILE = 16

REWARD_SCALE = 2.0
LOSS_SCALE = 4096.0
EPSILON = 1e-06
MESH = pl.DeviceIdType.MESH
F32 = jnp.float32
BF16 = jnp.bfloat16
VMEM_LIMIT = 56 * 1024 * 1024

PARTS = ((0, 0, 8, LMAX), (D, 8, 12, SEQ), (2 * D, 20, 12, SEQ))

ANY = pl.BlockSpec(memory_space=pl.ANY)
VMEM = pl.BlockSpec(memory_space=pltpu.VMEM)
SMEM = pl.BlockSpec(memory_space=pltpu.SMEM)


def place():
    rank = lax.axis_index("dp")
    return lax.div(rank, NY * NC), lax.rem(lax.div(rank, NC), NY), lax.rem(rank, NC), lax.axis_index("fsdp")


def device(z, y, c, x):
    return ((z * NY + y) * NC + c, x)


def remote(src, dst, send, recv, target):
    return pltpu.make_async_remote_copy(
        src_ref=src, dst_ref=dst, send_sem=send, recv_sem=recv, device_id=target, device_id_type=MESH
    )


def dot(a, b, left, right):
    return lax.dot_general(a, b, (((left,), (right,)), ((), ())), preferred_element_type=F32)


def rows_of(start, size, step):
    return pl.ds(pl.multiple_of(start, step), size)


def longest(sizes, dev):
    return jnp.where(sizes[2 * dev] >= sizes[2 * dev + 1], 0, 1)


def anchor_of(errors, reference):
    flat = errors[...].reshape(DP * NX, 128)
    total = jnp.sum(jnp.sum(flat, axis=0, keepdims=True), axis=1, keepdims=True)
    known = jnp.sum(jnp.sum(reference[...], axis=0, keepdims=True), axis=1, keepdims=True)
    return REWARD_SCALE * (known - total) / IMAGES


def loss_of(error_row, slot, known, liked, anchor):
    lane = lax.broadcasted_iota(jnp.int32, (1, 128), 1)
    error = jnp.sum(jnp.where(lane == slot, error_row, 0.0), axis=1, keepdims=True)
    sign = jnp.full((1, 1), 2 * liked - 1, jnp.int32).astype(F32)
    reward = REWARD_SCALE * (jnp.full((1, 1), known, F32) - error)
    sig = jax.nn.sigmoid(sign * (reward - anchor))
    return 1.0 - sig, LOSS_SCALE * REWARD_SCALE * sign * sig * (1.0 - sig)


def partners(z, y, c):
    near = [lax.rem(y + k // NC, NY) * NC + lax.rem(c + k % NC, NC) for k in range(NY * NC)]

    def each(act):
        for place_in in near[1:]:
            act(z * (NY * NC) + place_in)

        def step(dz, carry):
            base = lax.rem(z + dz, NZ) * (NY * NC)
            for place_in in near:
                act(base + place_in)
            return carry

        lax.fori_loop(1, NZ, step, 0)

    return each


def spread(stage, landed, sems, rank, x, each):
    def send(goal):
        remote(stage.at[goal], landed.at[rank], sems.at[0], sems.at[1], (goal, x)).start()

    each(send)
    landed[rank] = stage[rank]
    most = pl.ds(0, DP - 1)
    return remote(stage.at[most], landed.at[most], sems.at[0], sems.at[1], (lax.rem(rank + 1, DP), x))


def pick(landed, stage, senders):
    def step(n, carry):
        for d in range(4):
            stage[4 * n + d] = landed[jnp.maximum(senders[4 * n + d], 0)]
        return carry

    lax.fori_loop(0, DP // 4, step, 0)


def step_kernel(
    proj_hbm, resid_hbm, weight_hbm, target, final, modulation, reference, sizes, steps, liked, known, senders,
    grads_hbm, errors, out, losses, factors, info,
    grads, proj, resid, weight, attention, branch, d_mixed, mixed, d_branch,
    stage_a, first_a0, first_a1, second_a, final_a, stage_d, first_d, second_d, final_d, stage_g, first_g, second_g, final_g,
    scaled, term, core_send, core_recv, own, far_send, far_recv, near_send, near_recv, y_total,
    far_send_2, far_recv_2, near_send_2, near_recv_2, z_send, z_recv,
    load_sem, save_sem, w_send, w_recv, e_sems, move_sems, c_sems, r_sems, z_sems,
):
    z, y, c, x = place()
    rank = lax.axis_index("dp")
    dev = rank * NX + x
    sibling = device(z, y, 1 - c, x)
    right, left = (x + 1) % NX, (x + NX - 1) % NX
    opposite = (x + 2) % NX
    right_y, left_y = (y + 1) % NY, (y + NY - 1) % NY
    others_x = [device(z, y, c, (x + k) % NX) for k in range(1, NX)]
    others_z = [device((z + k) % NZ, y, c, x) for k in range(1, NZ)]
    x_pair = (device(z, y, c, right), device(z, y, c, left))
    y_pair = (device(z, right_y, c, x), device(z, left_y, c, x))
    sent = []

    load_proj = pltpu.make_async_copy(proj_hbm, proj, load_sem.at[0])
    load_proj.start()
    load_resid = pltpu.make_async_copy(resid_hbm.at[:, pl.ds(TXT, LMAX)], resid, load_sem.at[1])
    load_resid.start()
    load_weight = pltpu.make_async_copy(weight_hbm, weight.at[x], load_sem.at[2])
    load_weight.start()

    barrier = pltpu.get_barrier_semaphore()
    for partner in others_x:
        pl.semaphore_signal(barrier, inc=1, device_id=partner, device_id_type=MESH)

    each = partners(z, y, c)
    each(lambda goal: pl.semaphore_signal(barrier, inc=1, device_id=(goal, x), device_id_type=MESH))

    load_proj.wait()
    first = longest(sizes, dev)
    narrow = 2 * HD
    for s in range(2):
        for pair in range(2):
            cols = (2 * s + pair) * narrow
            for base, low, count, rows in PARTS:
                block = proj[first, SEQ - rows :, base + cols : base + cols + narrow]
                stage_a[s, pair * 32 + low : pair * 32 + low + count] = block.reshape(count, TILE, narrow)
    pl.semaphore_wait(barrier, DP - 1 + NX - 1)

    half = rows_of(c * HALF, HALF, 16)
    upper = rows_of(c * HALF, HALF // 2, 16)
    lower = rows_of(c * HALF + HALF // 2, HALF // 2, 16)
    mine = weight_hbm.at[half]
    to_right = remote(mine, weight.at[x, half], w_send.at[0], w_recv.at[0], x_pair[0])
    to_left = remote(mine, weight.at[x, half], w_send.at[1], w_recv.at[1], x_pair[1])
    to_right.start()
    to_left.start()

    def move(stage, landed, number):
        copy = spread(stage, landed, move_sems.at[number], rank, x, each)
        sent.append(copy)
        return copy

    first_a = (first_a0, first_a1)
    move_1a = [move(stage_a.at[s], first_a[s], s) for s in range(2)]
    move_2a = []

    def second_hop_a(s):
        move_1a[s].wait_recv()
        pick(first_a[s], second_a.at[s], senders)
        move_2a.append(move(second_a.at[s], final_a.at[s], 2 + s))

    root = 1.0 / math.sqrt(HD)
    key_index = lax.broadcasted_iota(jnp.int32, (LMAX, SEQ), 1)

    def softmax(q, k, size):
        scores = dot(q, k, 1, 1) * root
        scores = jnp.where(key_index < TXT + size, scores, -1e30)
        raised = jnp.exp(scores - jnp.max(scores, axis=-1, keepdims=True))
        return raised * (1.0 / jnp.sum(raised, axis=-1, keepdims=True))

    def gradients(q, k, v, probs, d_head):
        d_probs = dot(d_head, v, 1, 1)
        totals = jnp.sum(probs * d_probs, axis=-1, keepdims=True)
        d_scores = (probs * (d_probs - totals) * root).astype(BF16)
        return (
            dot(d_scores, k, 1, 0).astype(BF16),
            dot(d_scores, q, 0, 0).astype(BF16),
            dot(probs.astype(BF16), d_head, 0, 0).astype(BF16),
        )

    def rows_and_cols(i, h):
        cols = h * HD if isinstance(h, int) else pl.multiple_of(h * HD, HD)
        return rows_of(i * LMAX, LMAX, 16), pl.ds(cols, HD), cols

    def head_inputs(slot, cols):
        q = proj[slot, pl.ds(TXT, LMAX), pl.ds(cols, HD)]
        k = proj[slot, :, pl.ds(D + cols, HD)]
        v = proj[slot, :, pl.ds(2 * D + cols, HD)]
        return q, k, v

    def forward_group(n, carry):
        i = n // (HEADS // GROUP)
        slot = jnp.where(i == 0, first, 1 - first)
        size = sizes[2 * dev + slot]
        for j in range(GROUP):
            h = (n % (HEADS // GROUP)) * GROUP + j
            rows, out_cols, cols = rows_and_cols(i, h)
            q, k, v = head_inputs(slot, cols)
            probs = softmax(q, k, size)
            attention[i, h] = probs
            mixed[rows, out_cols] = dot(probs.astype(BF16), v, 1, 0).astype(BF16)
        return carry

    lax.fori_loop(0, 2 * HEADS // GROUP, forward_group, 0)

    to_right.wait_recv()
    on_right = remote(weight.at[left, upper], weight.at[left, upper], w_send.at[2], w_recv.at[2], x_pair[0])
    on_right.start()
    to_left.wait_recv()
    on_left = remote(weight.at[right, lower], weight.at[right, lower], w_send.at[3], w_recv.at[3], x_pair[1])
    on_left.start()
    across = []
    for n, owner in enumerate((left, right)):
        copy = remote(weight.at[owner, half], weight.at[owner, half], w_send.at[4 + n], w_recv.at[4 + n], sibling)
        copy.start()
        across.append(copy)
    load_weight.wait()
    load_resid.wait()

    def branch_part(owner):
        cols = rows_of(owner * COLS, COLS, 128)
        branch[:, cols] = dot(mixed[...], weight[owner], 1, 0)

    branch_part(x)
    second_hop_a(0)
    across[0].wait_recv()
    branch_part(left)
    across[1].wait_recv()
    branch_part(right)
    on_right.wait_recv()
    on_left.wait_recv()
    last = remote(weight.at[opposite, half], weight.at[opposite, half], w_send.at[6], w_recv.at[6], sibling)
    last.start()
    last.wait_recv()
    branch_part(opposite)
    sent.extend([to_right, to_left, on_right, on_left, last] + across)

    lane = lax.broadcasted_iota(jnp.int32, (1, 128), 1)
    row_index = lax.broadcasted_iota(jnp.int32, (PATCH, LMAX), 1)
    level = lax.broadcasted_iota(jnp.int32, (16, 32), 1)

    def image_middle(i, found):
        slot = jnp.where(i == 0, first, 1 - first)
        size = sizes[2 * dev + slot]
        chosen = dot((level == steps[2 * dev + slot]).astype(F32).astype(BF16), modulation[...], 1, 0)[0:1]
        gate = chosen[:, :D]
        shift = chosen[:, D : 2 * D]
        scale = 1.0 + chosen[:, 2 * D :]
        rows = rows_of(i * LMAX, LMAX, 16)
        residual = resid[slot].astype(F32) + gate * branch[rows]
        centered = residual - jnp.mean(residual, axis=-1, keepdims=True)
        inverse = lax.rsqrt(jnp.mean(centered * centered, axis=-1, keepdims=True) + EPSILON)
        unit = centered * inverse
        normed = (unit * scale + shift).astype(BF16)
        predicted = dot(final[...], normed, 1, 1)
        differ = jnp.where(row_index < size, predicted - target[slot].astype(F32), 0.0)
        divisor = jnp.full((1, 1), PATCH * size, jnp.int32).astype(F32)
        squares = jnp.sum(jnp.sum(differ * differ, axis=1, keepdims=True), axis=0, keepdims=True)
        d_predicted = (differ * (2.0 / divisor)).astype(BF16)
        d_normed = dot(d_predicted, final[...], 0, 0) * scale
        d_residual = inverse * (
            d_normed
            - jnp.mean(d_normed, axis=-1, keepdims=True)
            - unit * jnp.mean(d_normed * unit, axis=-1, keepdims=True)
        )
        d_branch[rows, :] = (gate * d_residual).astype(BF16)
        return found + jnp.where(lane == slot, squares / divisor, 0.0)

    errors[rank, x] = lax.fori_loop(0, 2, image_middle, jnp.zeros((1, 128), F32))

    def hear(copies):
        for copy in copies:
            copy.wait_recv()

    e_x = [
        remote(errors.at[rank, x], errors.at[rank, x], e_sems.at[0, k], e_sems.at[1, k], goal)
        for k, goal in enumerate(others_x)
    ]
    for copy in e_x:
        copy.start()
    sent.extend(e_x)
    second_hop_a(1)

    total = dot(d_branch[:, pl.ds(0, COLS)], weight[0], 1, 1)
    for owner in range(1, NX):
        total += dot(d_branch[:, pl.ds(owner * COLS, COLS)], weight[owner], 1, 1)
    d_mixed[...] = total.astype(BF16)

    hear(e_x)
    each(
        lambda goal: remote(
            errors.at[rank], errors.at[rank], e_sems.at[0, NX - 1], e_sems.at[1, NX - 1], (goal, x)
        ).start()
    )
    most = pl.ds(0, DP - 1)
    e_all = remote(errors.at[most], errors.at[most], e_sems.at[0, NX - 1], e_sems.at[1, NX - 1], sibling)
    sent.append(e_all)

    for h in range(EARLY):
        for n in range(LMAX // TILE):
            stage_d[n * EARLY + h] = d_mixed[pl.ds(n * TILE, TILE), pl.ds(h * HD, HD)]
    move_1d = move(stage_d, first_d, 4)

    def store(i, h, blocks):
        side, out_cols = h // (HEADS // 2), rows_of((h % (HEADS // 2)) * HD, HD, HD)
        for (_, low, count, _), block in zip(PARTS, blocks):
            grads[i, side, low : low + count, :, out_cols] = block.reshape(count, TILE, HD)

    def head_backward(i, slot, h):
        rows, in_cols, cols = rows_and_cols(i, h)
        blocks = gradients(*head_inputs(slot, cols), attention[i, h], d_mixed[rows, in_cols])
        store(i, h, blocks)
        return blocks

    for h in range(EARLY, HEADS):
        blocks = head_backward(0, first, h)
        pair, place_in = (h - EARLY) // 2, pl.ds((h - EARLY) % 2 * HD, HD)
        for (_, low, count, _), block in zip(PARTS, blocks):
            stage_g[pair * 32 + low : pair * 32 + low + count, :, place_in] = block.reshape(count, TILE, HD)
    move_1g = move(stage_g, first_g, 5)
    e_all.wait_recv()

    anchor = anchor_of(errors, reference)
    origin = senders[rank]
    from_rank = jnp.maximum(origin, 0)
    from_dev = from_rank * NX + x
    from_slot = longest(sizes, from_dev)
    third_size = sizes[2 * from_dev + from_slot]

    def judge(row, slot, index):
        return loss_of(row, slot, known[index], liked[index], anchor)

    row = errors[rank, x]
    judged = [judge(row, slot, 2 * dev + slot) for slot in range(2)]
    judged.append(
        judge(
            errors[from_rank, x], from_slot, 2 * from_dev + from_slot
        )
    )
    for slot in range(3):
        loss, slope = judged[slot]
        here = origin >= 0 if slot == 2 else jnp.logical_or(origin >= 0, first != slot)
        losses[slot] = jnp.where(here, loss[0, 0], 0.0)
        factors[slot] = slope[0, 0]
        info[slot] = 2 if slot == 2 else jnp.where(first == slot, 0, 1)
        info[3 + slot] = jnp.where(here, 1, 0)

    for i in range(2):
        slope = jnp.where(first == i, judged[0][1], judged[1][1])
        rows = pl.ds(i * LMAX, LMAX)
        scaled[rows, :] = (d_branch[rows, :].astype(F32) * slope).astype(BF16)

    def make(owner):
        term[...] = dot(mixed[...], scaled[:, rows_of(owner * COLS, COLS, 128)], 0, 0)
        for p in range(2):
            for yy in range(NY):
                for core, goal in ((1 - c, core_send), (c, own)):
                    parts = [
                        term[rows_of(((zz * NY + yy) * NC + core) * PART, PART, 8), :]
                        for zz in range(p * NZ // 2, (p + 1) * NZ // 2)
                    ]
                    block = jnp.concatenate(parts, axis=0)
                    goal[owner, pl.ds((p * NY + yy) * STRIP, STRIP), :] = block.astype(goal.dtype)
        copy = remote(core_send.at[owner], core_recv.at[owner], c_sems.at[0, owner], c_sems.at[1, owner], sibling)
        copy.start()
        return copy

    owners = (opposite, right, left, x)
    copies = [make(owner) for owner in owners]
    sent.extend(copies)

    def chip_total(n):
        copies[n].wait_recv()
        own[owners[n]] = own[owners[n]] + core_recv[owners[n]].astype(F32)

    def ring_far(number, pair, block, bufs):
        far_out, far_in, _, _ = bufs
        outer = []
        for n in range(2):
            far_out[n] = block(n).astype(BF16)
            copy = remote(far_out.at[n], far_in.at[n], r_sems.at[number, 0, n], r_sems.at[number, 1, n], pair[n])
            copy.start()
            outer.append(copy)
        sent.extend(outer)
        return outer

    def ring_near(number, pair, outer, blocks, bufs):
        _, far_in, near_out, near_in = bufs
        middle = far_in.shape[1]
        inner = []
        for n in range(2):
            outer[n].wait_recv()
            for part in range(2):
                piece = blocks[n](part)
                if part == n:
                    piece = piece + far_in[n].astype(F32)
                near_out[n, pl.ds(part * middle, middle), :] = piece.astype(BF16)
            copy = remote(
                near_out.at[n], near_in.at[n], r_sems.at[number, 0, 2 + n], r_sems.at[number, 1, 2 + n], pair[n]
            )
            copy.start()
            inner.append(copy)
        sent.extend(inner)
        return inner

    def x_first(owner):
        return lambda part: own[owner, pl.ds(part * (BLOCK // 2), BLOCK // 2), :]

    def y_strip(which):
        return rows_of(BLOCK + which * STRIP, STRIP, 16)

    def y_first(which):
        return lambda part: jnp.concatenate([own[2 * part + n, y_strip(which), :] for n in range(2)], axis=0)

    def y_second(which):
        return lambda part: own[x, rows_of(which * STRIP + part * (STRIP // 2), STRIP // 2, 16), :]

    def x_second(owner):
        return lambda part: own[owner, rows_of(BLOCK + y * STRIP + part * (STRIP // 2), STRIP // 2, 16), :]

    bufs = [(far_send.at[n], far_recv.at[n], near_send.at[n], near_recv.at[n]) for n in range(2)]
    small = [(far_send_2.at[n], far_recv_2.at[n], near_send_2.at[n], near_recv_2.at[n]) for n in range(2)]
    chip_total(0)
    outer_x = ring_far(0, x_pair, x_first(opposite), bufs[0])
    chip_total(1)
    chip_total(2)
    chip_total(3)
    outer_y = ring_far(1, y_pair, y_first((y + 2) % NY), bufs[1])

    def backward(i, slot, groups):
        def group(n, carry):
            for j in range(GROUP):
                head_backward(i, slot, n * GROUP + j)
            return carry

        lax.fori_loop(0, groups, group, 0)

    backward(0, first, EARLY // GROUP)
    save = [pltpu.make_async_copy(grads.at[i], grads_hbm.at[i], save_sem.at[i]) for i in range(3)]
    save[0].start()
    inner_x = ring_near(0, x_pair, outer_x, (x_first(right), x_first(left)), bufs[0])
    inner_y = ring_near(1, y_pair, outer_y, (y_first(right_y), y_first(left_y)), bufs[1])
    backward(1, 1 - first, HEADS // GROUP)
    save[1].start()

    def third_rows(h, part):
        _, low, count, rows = PARTS[part]
        base = h % 4 // 2 * 32 + low
        return final_a[h // 4, base : base + count, :, pl.ds(h % 2 * HD, HD)].reshape(rows, HD)

    for s in range(2):
        move_2a[s].wait_recv()
        for h in range(4 * s, 4 * s + 4):
            attention[0, h] = softmax(third_rows(h, 0), third_rows(h, 1), third_size)

    move_1d.wait_recv()
    pick(first_d, second_d, senders)
    move_2d = move(second_d, final_d, 6)

    hear(inner_x)
    whole = pl.ds(0, BLOCK)
    own[x, whole, :] = own[x, whole, :] + near_recv[0, 0].astype(F32) + near_recv[0, 1].astype(F32)
    outer_y2 = ring_far(2, y_pair, y_second((y + 2) % NY), small[0])
    hear(inner_y)
    for owner in range(NX):
        rows = pl.ds(owner * STRIP, STRIP)
        own[owner, y_strip(y), :] = (
            own[owner, y_strip(y), :] + near_recv[1, 0, rows, :].astype(F32) + near_recv[1, 1, rows, :].astype(F32)
        )
    outer_x2 = ring_far(3, x_pair, x_second(opposite), small[1])

    move_1g.wait_recv()
    pick(first_g, second_g, senders)
    move_2g = move(second_g, final_g, 7)

    inner_y2 = ring_near(2, y_pair, outer_y2, (y_second(right_y), y_second(left_y)), small[0])
    inner_x2 = ring_near(3, x_pair, outer_x2, (x_second(right), x_second(left)), small[1])
    hear(inner_y2 + inner_x2)
    for p, rows in enumerate((rows_of(y * STRIP, STRIP, 16), y_strip(y))):
        y_total[pl.ds(p * STRIP, STRIP), :] = (
            own[x, rows, :] + near_recv_2[p, 0].astype(F32) + near_recv_2[p, 1].astype(F32)
        )
    for zz in range(NZ):
        block = jnp.concatenate([y_total[pl.ds(zz * PART, PART), :], jnp.zeros((8, COLS), F32)], axis=0)
        z_send[zz] = block.astype(BF16)
    z_copies = []
    for k in range(1, NZ):
        copy = remote(
            z_send.at[(z + k) % NZ], z_recv.at[k - 1], z_sems.at[0, k - 1], z_sems.at[1, k - 1], others_z[k - 1]
        )
        copy.start()
        z_copies.append(copy)
    sent.extend(z_copies)

    move_2d.wait_recv()
    for h in range(EARLY):
        d_head = jnp.concatenate([final_d[n * EARLY + h] for n in range(LMAX // TILE)], axis=0)
        store(2, h, gradients(*[third_rows(h, part) for part in range(3)], attention[0, h], d_head))

    total = y_total[rows_of(z * PART, PART, 8), :]
    for k, copy in enumerate(z_copies):
        copy.wait_recv()
        total = total + z_recv[k].astype(F32)[:PART]
    out[...] = total

    move_2g.wait_recv()
    for h in range(EARLY, HEADS):
        pair, place_in = (h - EARLY) // 2, pl.ds((h - EARLY) % 2 * HD, HD)
        out_cols = pl.ds((h % (HEADS // 2)) * HD, HD)
        grads[2, h // (HEADS // 2), :, :, out_cols] = final_g[pair * 32 : pair * 32 + 32, :, place_in]
    save[2].start()
    for copy in sent:
        copy.wait_send()
    for copy in save:
        copy.wait()


def step_pass(
    projections, residual_in, velocity_target, out_weight, final_weight, modulation,
    reference, sizes, steps, liked, known, senders,
):
    stack = (3, 2, 32, TILE, HEADS // 2 * HD)
    both = pltpu.VMEM((2, DP, TILE, 2 * HD), BF16)
    one = pltpu.VMEM((DP, TILE, 2 * HD), BF16)
    early = [both, one, one, both, both]
    middle = [pltpu.VMEM((DP, TILE, HD), BF16)] * 4
    late = [pltpu.VMEM((DP, TILE, 2 * HD), BF16)] * 4
    return pl.pallas_call(
        step_kernel,
        name="step",
        out_shape=(
            jax.ShapeDtypeStruct(stack, BF16),
            jax.ShapeDtypeStruct((DP, NX, 1, 128), F32),
            jax.ShapeDtypeStruct((PART, COLS), F32),
            jax.ShapeDtypeStruct((3,), F32),
            jax.ShapeDtypeStruct((3,), F32),
            jax.ShapeDtypeStruct((6,), jnp.int32),
        ),
        in_specs=[ANY, ANY, ANY, VMEM, VMEM, VMEM, VMEM] + [SMEM] * 5,
        out_specs=(ANY, VMEM, VMEM, SMEM, SMEM, SMEM),
        scratch_shapes=[
            pltpu.VMEM(stack, BF16),
            pltpu.VMEM((2, SEQ, 3 * D), BF16),
            pltpu.VMEM((2, LMAX, D), BF16),
            pltpu.VMEM((NX, D, COLS), BF16),
            pltpu.VMEM((2, HEADS, LMAX, SEQ), F32),
            pltpu.VMEM((2 * LMAX, D), F32),
            pltpu.VMEM((2 * LMAX, D), BF16),
            pltpu.VMEM((2 * LMAX, D), BF16),
            pltpu.VMEM((2 * LMAX, D), BF16),
            *early,
            *middle,
            *late,
            pltpu.VMEM((2 * LMAX, D), BF16),
            pltpu.VMEM((D, COLS), F32),
            pltpu.VMEM((NX, HALF, COLS), BF16),
            pltpu.VMEM((NX, HALF, COLS), BF16),
            pltpu.VMEM((NX, HALF, COLS), F32),
            *[pltpu.VMEM((2, 2, BLOCK // 2, COLS), BF16)] * 2,
            *[pltpu.VMEM((2, 2, BLOCK, COLS), BF16)] * 2,
            pltpu.VMEM((2 * STRIP, COLS), F32),
            *[pltpu.VMEM((2, 2, STRIP // 2, COLS), BF16)] * 2,
            *[pltpu.VMEM((2, 2, STRIP, COLS), BF16)] * 2,
            pltpu.VMEM((NZ, PART + 8, COLS), BF16),
            pltpu.VMEM((NZ - 1, PART + 8, COLS), BF16),
            pltpu.SemaphoreType.DMA((3,)),
            pltpu.SemaphoreType.DMA((3,)),
            pltpu.SemaphoreType.DMA((7,)),
            pltpu.SemaphoreType.DMA((7,)),
            pltpu.SemaphoreType.DMA((2, NX)),
            pltpu.SemaphoreType.DMA((8, 2)),
            pltpu.SemaphoreType.DMA((2, NX)),
            pltpu.SemaphoreType.DMA((4, 2, 4)),
            pltpu.SemaphoreType.DMA((2, NZ - 1)),
        ],
        compiler_params=pltpu.CompilerParams(
            collective_id=0, has_side_effects=True, vmem_limit_bytes=VMEM_LIMIT
        ),
        cost_estimate=pl.CostEstimate(flops=5_700_000_000, bytes_accessed=20_000_000, transcendentals=800_000),
    )(
        projections, residual_in, out_weight, velocity_target, final_weight, modulation,
        reference, sizes, steps, liked, known, senders,
    )


def place_kernel(info, factors, grads, out):
    slot = pl.program_id(0)
    wide = HEADS // 2 * HD

    @pl.when(info[3 + slot] == 0)
    def _():
        out[...] = jnp.zeros_like(out)

    @pl.when(info[3 + slot] == 1)
    def _():
        slope = jnp.full((1, 1), factors[slot], F32)
        for side in range(2):
            for base, low, count, rows in PARTS:
                block = grads[0, side, low : low + count].reshape(rows, wide).astype(F32) * slope
                out[0, SEQ - rows :, base + side * wide : base + (side + 1) * wide] = block.astype(BF16)
        out[0, :TXT, :D] = jnp.zeros((TXT, D), BF16)


def place_pass(info, factors, grads):
    return pl.pallas_call(
        place_kernel,
        name="slots",
        out_shape=jax.ShapeDtypeStruct((3, SEQ, 3 * D), BF16),
        grid_spec=pltpu.PrefetchScalarGridSpec(
            num_scalar_prefetch=2,
            grid=(3,),
            in_specs=[pl.BlockSpec((1, *grads.shape[1:]), lambda i, info, factors: (info[i], 0, 0, 0, 0))],
            out_specs=pl.BlockSpec((1, SEQ, 3 * D), lambda i, info, factors: (i, 0, 0)),
        ),
        compiler_params=pltpu.CompilerParams(vmem_limit_bytes=VMEM_LIMIT),
        cost_estimate=pl.CostEstimate(flops=3_000_000, bytes_accessed=10_000_000, transcendentals=10),
    )(info, factors, grads)


def local(
    projections, residual_in, velocity_target, out_weight, final_weight, modulation,
    bucket_sizes, liked, timesteps, reference_error, move_list,
):
    goal = jnp.arange(DP, dtype=jnp.int32)[:, None] == move_list[0, :, 1][None, :]
    senders = jnp.sum(jnp.where(goal, move_list[0, :, 0][None, :] + 1, 0), axis=1) - 1
    grads, _, weight_grad, slot_loss, factors, info = step_pass(
        projections, residual_in, jnp.swapaxes(velocity_target, 1, 2), out_weight, final_weight.T,
        modulation, reference_error.reshape(4, 128), bucket_sizes, timesteps, liked, reference_error, senders,
    )
    return (weight_grad, place_pass(info, factors, grads), slot_loss)


def solution(mesh):
    in_specs = (
        P(("dp", "fsdp"), None, None),
        P(("dp", "fsdp"), None, None),
        P(("dp", "fsdp"), None, None),
        P(None, "fsdp"),
        P(),
        P(),
        P(),
        P(),
        P(),
        P(),
        P("fsdp", None, None),
    )
    out_specs = (P("dp", "fsdp"), P(("dp", "fsdp"), None, None), P(("dp", "fsdp")))
    return jax.shard_map(local, mesh=mesh, in_specs=in_specs, out_specs=out_specs, check_vma=False)
```
